32 devices in a mesh: row: 8 (over y, x, core), col: 4 (over z).
Axes of the slice: x: 2, y: 2, z: 4, core: 2. Of those that a mesh axis runs over, the one named last changes fastest.
Arguments:
- x_blocks: bfloat16 [128, 8, 2, 128, 128], P('row', 'col'), may hold values from -1.796875 to 1.796875
- x_columns: int32 [128, 8, 2], P('row', 'col'), may hold values from 0 to 95, as said below
- kept_columns: int32 [768, 8], P('row', 'col'), may hold values from 0 to 191, as said below
Outputs:
- result_blocks: float32 [768, 8, 128, 128], P('row', 'col')
The draws below stay inside these ranges and needn't reach their ends.
Inputs may be any that keep to these rules, and one draw needn't show every extreme that they name: `x_columns`: the 2 entries of one block row and one group are distinct. `kept_columns`: the 2 entries of one result block row within one column panel are distinct.
All inputs are finite; a program needn't handle non-finite values.
Results may differ from the reference program's by a relative error of at most 0.0003.
Values may be sent and summed in bfloat16 or wider, within the bound.
No kernel may reach another device: no remote copies, remote signals or barrier semaphores. Data moves between devices by JAX's collectives and lax.ppermute only.
A program may use at most 320 MiB of HBM per device.

```python
import jax
import jax.numpy as jnp
from jax import lax

BS = 128
GW = 96
E = 2
F = 2
BROWS = 128
GROUPS = 8
GPANEL = 2
N_COL = 4


def shared_columns(key):
    col_key = jax.random.fold_in(key, 31)
    scores = jax.random.randint(col_key, (BROWS, GROUPS, GW), 0, 2 ** 16) * GW
    scores = scores + lax.broadcasted_iota(jnp.int32, (BROWS, GROUPS, GW), 2)
    _, picked = lax.top_k(scores, E)
    return picked.astype(jnp.int32)


def draw_x_columns(key, part):
    return shared_columns(key)


def draw_kept_columns(key, part):
    columns = shared_columns(key)
    rows_all = GROUPS * GW
    local_pos = lax.broadcasted_iota(jnp.int32, (GW,), 0)
    by_group = columns.transpose(1, 0, 2)
    cover = jnp.any(by_group[:, None, :, :] == local_pos[None, :, None, None], axis=3).reshape(rows_all, BROWS)
    row_scores = jax.random.randint(jax.random.fold_in(key, 32), (rows_all, N_COL, BROWS), 0, 2 ** 14) * BROWS
    row_scores = row_scores + lax.broadcasted_iota(jnp.int32, (rows_all, N_COL, BROWS), 2)
    masked = jnp.where(cover[:, None, :], row_scores, -1)
    best, chosen = lax.top_k(masked, 1)
    has_cover = best[:, :, 0] >= 0
    picked_rows = jnp.take(columns, chosen[:, :, 0].astype(jnp.int32), axis=0)
    picked_rows = picked_rows.reshape(rows_all, N_COL, N_COL, GPANEL, E)
    same_panel = lax.broadcasted_iota(jnp.int32, (N_COL, N_COL), 0) == lax.broadcasted_iota(jnp.int32, (N_COL, N_COL), 1)
    in_panel = jnp.sum(jnp.where(same_panel[None, :, :, None, None], picked_rows, 0), axis=2)
    group_base = lax.broadcasted_iota(jnp.int32, (GPANEL,), 0) * GW
    candidates = (in_panel + group_base[None, None, :, None]).reshape(rows_all, N_COL, GPANEL * E)
    pick_scores = jax.random.randint(jax.random.fold_in(key, 33), (rows_all, N_COL, GPANEL * E), 0, 2 ** 16) * (GPANEL * E)
    pick_scores = pick_scores + lax.broadcasted_iota(jnp.int32, (rows_all, N_COL, GPANEL * E), 2)
    _, order = lax.top_k(pick_scores, F)
    from_row = jnp.take_along_axis(candidates, order.astype(jnp.int32), axis=2)
    start = jax.random.randint(jax.random.fold_in(key, 34), (rows_all, N_COL, 1), 0, GPANEL * GW)
    spare = (start + lax.broadcasted_iota(jnp.int32, (1, 1, F), 2)) % (GPANEL * GW)
    kept = jnp.where(has_cover[:, :, None], from_row, spare)
    return kept.reshape(rows_all, N_COL * F).astype(jnp.int32)


def block_scale(stream_key, extent, cuts, least, high):
    def one(axis_at, blocks):
        heights = jax.random.uniform(jax.random.fold_in(jax.random.fold_in(stream_key, 6), axis_at), (blocks,), jnp.float32, least / len(cuts), high / len(cuts))
        return jnp.repeat(jnp.exp(heights), extent[axis_at] // blocks).reshape((-1,) + (1,) * (len(extent) - axis_at - 1))

    factor_of = one(*cuts[0])
    for cut in cuts[1:]:
        factor_of = factor_of * one(*cut)
    return factor_of


def bell_draw(key, extent, width, reach, cuts=(), held_as=jnp.bfloat16):
    values = jax.random.normal(key, extent, jnp.float32) * width
    if len(cuts) > 0:
        values = block_scale(key, extent, cuts, -0.22, 0.18) * values
    return jnp.clip(values, min=-reach, max=reach).astype(held_as)


def setup_inputs(seed: int = 0) -> dict:
    splits = jax.random.split(jax.random.key(seed), 4)
    return {
        "x_blocks": bell_draw(splits[0], (BROWS, GROUPS, E, BS, BS), 0.3, 1.796875, ((0, 8), (1, 4))),
        "x_columns": draw_x_columns(jax.random.fold_in(splits[3], 71), 0),
        "kept_columns": draw_kept_columns(jax.random.fold_in(splits[3], 71), 0),
    }


def reference(x_blocks, x_columns, kept_columns):
    brows, groups, slots = x_columns.shape
    block_size = x_blocks.shape[-1]
    per_row = N_COL * F
    gpanel = groups // N_COL
    block_count = groups * slots
    group_of = jnp.repeat(jnp.arange(groups, dtype=jnp.int32), slots)
    total_slots = groups * GW * per_row
    panel_of = group_of // gpanel

    def scan_step(accumulated, row_pair):
        row_values, row_cols = row_pair
        flat_v = row_values.reshape(block_count, block_size, block_size).astype(jnp.float32)
        flat_c = row_cols.reshape(block_count).astype(jnp.int32)
        products = jnp.einsum("ati,btj->abij", flat_v, flat_v)
        out_row = group_of * GW + flat_c
        in_panel = (group_of % gpanel) * GW + flat_c
        kept_rows = jnp.take(kept_columns, out_row, axis=0).reshape(block_count, N_COL, F)
        chosen = kept_rows[:, panel_of, :]
        matches = chosen == in_panel[None, :, None]
        is_hit = jnp.any(matches, axis=2)
        slot_pick = jnp.sum(jnp.where(matches, jnp.arange(F, dtype=jnp.int32)[None, None, :], 0), axis=2).astype(jnp.int32)
        target = jnp.where(is_hit, (out_row[:, None] * N_COL + panel_of[None, :]) * F + slot_pick, total_slots).astype(jnp.int32)
        accumulated = accumulated.at[target.reshape(-1)].add(products.reshape(-1, block_size, block_size), mode="drop")
        return accumulated, None

    zero_sums = jnp.zeros((total_slots, block_size, block_size), jnp.float32)
    accumulated, _ = lax.scan(scan_step, zero_sums, (x_blocks, x_columns))
    return accumulated.reshape(groups * GW, per_row, block_size, block_size)
```

```python
import functools

import jax
import jax.numpy as jnp
from jax import lax
from jax.experimental import pallas as pl
from jax.experimental.pallas import tpu as pltpu
from jax.sharding import PartitionSpec as P

SHIFT = 16
UNROLL = 8


def product_kernel(code_ref, place_ref, *refs, cuts, source_count, slot_count, group_count, first):
    chip_count, panel_slots = source_count // group_count, group_count * slot_count
    row0, row_count, pieces = cuts[0], cuts[-1] - cuts[0], list(zip(cuts, cuts[1:]))
    a_refs = []
    for _ in pieces:
        a_refs.append(refs[:source_count])
        refs = refs[source_count:]
    b_refs, refs = (refs[:source_count], refs[source_count : 2 * source_count]), refs[2 * source_count :]
    if not first:
        before_ref, refs = refs[0], refs[1:]
    out_ref, blocks, total, list_a, list_b, list_o, touched, seen, a_sem, b_sem, out_sem = refs
    own, group, panel = place_ref[0], place_ref[1], place_ref[2]
    a_size, b_size = row_count * slot_count, row_count * panel_slots
    b_base = source_count * a_size

    def a_part(source):
        return blocks.at[pl.ds(source * a_size, a_size)]

    def start_a(source):
        chip, side = source // group_count, source % group_count
        for piece, (i, j) in enumerate(pieces):
            at = source * a_size + (i - row0) * slot_count
            for row in range(j - i):
                held = a_refs[piece][side * chip_count + chip]
                held = held.at[panel] if len(held.shape) == 4 else held
                sent = held.at[pl.ds(row * panel_slots + group * slot_count, slot_count)]
                part = blocks.at[pl.ds(at + row * slot_count, slot_count)]
                pltpu.make_async_copy(sent, part, a_sem.at[source]).start()

    def wait_a(source):
        pltpu.make_async_copy(a_part(source), a_part(source), a_sem.at[source]).wait()

    half = b_refs[0][0].shape[0]
    b_start, b_end = row0 * panel_slots, (row0 + row_count) * panel_slots

    def b_copies(source):
        for at, (i, j) in enumerate(((b_start, min(b_end, half)), (max(b_start, half), b_end))):
            if i < j:
                sent = b_refs[at][source].at[pl.ds(i - at * half, j - i)]
                part = blocks.at[pl.ds(b_base + source * b_size + i - b_start, j - i)]
                yield pltpu.make_async_copy(sent, part, b_sem.at[at, source])

    def load(block):
        return pltpu.make_async_copy(before_ref.at[block], total.at[block], out_sem.at[block])

    def store(block):
        return pltpu.make_async_copy(total.at[block], out_ref.at[block], out_sem.at[block])

    for source in range(source_count):
        for copy in b_copies(source):
            copy.start()

    @pl.when(own == 0)
    def _():
        for source in range(source_count):
            start_a(source)

    block_total = out_ref.shape[0]
    keep_count = code_ref.shape[0] // (source_count * row_count * slot_count)
    if first:
        total[...] = jnp.zeros_like(total)
    else:

        def clear(block, carry):
            seen[block] = 0
            return carry

        lax.fori_loop(0, block_total, clear, 0)

    def note(at, counts):
        count, touched_count = counts
        row, slot = at // slot_count, at % slot_count
        kept_at = b_base + row * panel_slots + group * slot_count + slot
        a_at = jnp.where(own == 1, kept_at, at)
        for keep in range(keep_count):
            code = code_ref[at * keep_count + keep]
            block = lax.bitwise_and(code, (1 << SHIFT) - 1)
            list_a[count] = a_at
            list_b[count] = lax.shift_right_logical(code, SHIFT) + b_base
            list_o[count] = block
            count = count + (code >= 0).astype(jnp.int32)
            if not first:
                known = jnp.minimum(block, block_total - 1)
                fresh = jnp.logical_and(code >= 0, seen[known] == 0)
                touched[touched_count] = known

                @pl.when(fresh)
                def _():
                    seen[known] = 1
                    load(known).start()

                touched_count = touched_count + fresh.astype(jnp.int32)
        return count, touched_count

    count, touched_count = lax.fori_loop(
        0, source_count * row_count * slot_count, note, (jnp.int32(0), jnp.int32(0))
    )

    def each_touched(act):
        def step(at, carry):
            act(touched[at])
            return carry

        lax.fori_loop(0, touched_count, step, 0)

    for source in range(source_count):
        for copy in b_copies(source):
            copy.wait()

    @pl.when(own == 0)
    def _():
        for source in range(source_count):
            wait_a(source)

    if not first:
        each_touched(lambda block: load(block).wait())

    def product(at):
        a, b = blocks[list_a[at]], blocks[list_b[at]]
        return lax.dot_general(a, b, (((0,), (0,)), ((), ())), preferred_element_type=jnp.float32)

    def several(step, carry):
        at = step * UNROLL
        values = [product(at + k) for k in range(UNROLL)]
        for k in range(UNROLL):
            total[list_o[at + k]] += values[k]
        return carry

    for k in range(UNROLL):
        list_a[count + k] = b_base
        list_b[count + k] = b_base
        list_o[count + k] = block_total
    lax.fori_loop(0, (count + UNROLL - 1) // UNROLL, several, 0)
    if first:
        whole_store = pltpu.make_async_copy(total.at[pl.ds(0, block_total)], out_ref, out_sem.at[0])
        whole_store.start()
        whole_store.wait()
    else:
        each_touched(lambda block: store(block).start())
        each_touched(lambda block: store(block).wait())


def add_products(cuts, code, place, a_parts, b_parts, before, out_blocks, group_count, slot_count):
    source_count, block_size, row_count = len(b_parts) // 2, b_parts[0].shape[-1], cuts[-1] - cuts[0]
    pairs = code.shape[0]
    first = before is None
    anywhere = pl.BlockSpec(memory_space=pl.ANY)
    scalars = pl.BlockSpec(memory_space=pltpu.SMEM)
    operands = [code, place, *a_parts, *b_parts] + ([] if first else [before])
    block_count = source_count * row_count * (1 + group_count) * slot_count
    return pl.pallas_call(
        functools.partial(
            product_kernel,
            cuts=cuts,
            source_count=source_count,
            slot_count=slot_count,
            group_count=group_count,
            first=first,
        ),
        out_shape=jax.ShapeDtypeStruct((out_blocks, block_size, block_size), jnp.float32),
        in_specs=[scalars, scalars] + [anywhere] * (len(operands) - 2),
        out_specs=anywhere,
        scratch_shapes=[
            pltpu.VMEM((block_count, block_size, block_size), jnp.bfloat16),
            pltpu.VMEM((out_blocks + 1, block_size, block_size), jnp.float32),
            pltpu.SMEM((pairs + UNROLL,), jnp.int32),
            pltpu.SMEM((pairs + UNROLL,), jnp.int32),
            pltpu.SMEM((pairs + UNROLL,), jnp.int32),
            pltpu.SMEM((out_blocks + 1,), jnp.int32),
            pltpu.SMEM((out_blocks,), jnp.int32),
            pltpu.SemaphoreType.DMA((source_count,)),
            pltpu.SemaphoreType.DMA((2, source_count)),
            pltpu.SemaphoreType.DMA((out_blocks,)),
        ],
        input_output_aliases={} if first else {len(operands) - 1: 0},
        compiler_params=pltpu.CompilerParams(vmem_limit_bytes=52 << 20),
        cost_estimate=pl.CostEstimate(
            flops=2 * pairs * block_size**3,
            bytes_accessed=2 * block_count * block_size**2 + 8 * out_blocks * block_size**2,
            transcendentals=0,
        ),
    )(*operands)


def after(value, *others):
    return lax.optimization_barrier((value, *others))


def on_device(x_blocks, x_columns, kept_columns):
    rows_here, group_count, slot_count, block_size, _ = x_blocks.shape
    width_g, keep_count = kept_columns.shape
    n_row = lax.axis_size("row")
    n_col = lax.axis_size("col")
    row, col = lax.axis_index("row"), lax.axis_index("col")
    panel, group = row // group_count, row % group_count
    out_blocks = width_g * keep_count
    panel_slots = group_count * slot_count
    cuts = (0, rows_here * 8 // 16, rows_here * 13 // 16, rows_here)
    everyone = [(r, c) for r in range(n_row) for c in range(n_col)]

    def send(value, pairs):
        places = [(r * n_col + c, r2 * n_col + c2) for (r, c), (r2, c2) in pairs]
        return lax.ppermute(value, ("row", "col"), places)

    def to_row(value, offset, skip_panel=False):
        return send(
            value,
            [
                ((r, c), (r ^ offset, c))
                for r, c in everyone
                if not (skip_panel and (r ^ offset) // group_count == c)
            ],
        )

    x_flat = x_blocks.reshape(rows_here * panel_slots, block_size, block_size)
    first_part = x_flat[: cuts[1] * panel_slots]
    x_rest, first_part = after(x_flat, first_part)
    gathered = [lax.all_gather(first_part, "col")]
    for i, j in zip(cuts[1:], cuts[2:]):
        gathered.append(lax.all_gather(x_rest[i * panel_slots : j * panel_slots], "col"))
    tags = x_columns.reshape(rows_here, panel_slots).astype(jnp.bfloat16)
    tags = jnp.pad(tags, ((0, block_size - rows_here), (0, block_size - panel_slots)))
    half = rows_here * panel_slots // 2
    halves = [
        first_part if half == cuts[1] * panel_slots else x_flat[:half],
        jnp.concatenate([x_rest[half:], tags[None]]),
    ]

    chips = range(group_count, n_row, group_count)
    near = [offset for offset in chips if not (offset // group_count) & (offset // group_count - 1)]
    far = [offset for offset in chips if offset not in near]
    b_parts = [[part] + [None] * (n_row - 1) for part in halves]
    for at in range(2):
        for offset in near if at else near[::-1]:
            b_parts[at][offset] = to_row(halves[at], offset)
    for offset in sorted(far, key=lambda offset: bin(offset).count("1")):
        steps = [step for step in near if step & offset]
        for at, step in enumerate((steps[0], steps[-1])):
            b_parts[at][offset] = to_row(b_parts[at][offset ^ step], step)
    for at in range(2):
        for offset in (0, *near):
            for side in range(1, group_count):
                b_parts[at][offset + side] = to_row(b_parts[at][offset], side)
    there = [(at, offset) for at in range(2) for offset in range(n_row) if b_parts[at][offset] is not None]
    gathered[0], *arrived = after(gathered[0], *(b_parts[at][offset] for at, offset in there))
    for (at, offset), part in zip(there, arrived):
        b_parts[at][offset] = part
    for at in range(2):
        for offset in far:
            for side in range(1, group_count):
                b_parts[at][offset + side] = to_row(b_parts[at][offset], side)

    def pieces(q):
        return [
            lax.dynamic_index_in_dim(gathered[q], panel ^ (offset // group_count), 0, False) for offset in chips
        ]

    def in_plane(q, parts):
        return [gathered[q], *(to_row(part, offset, True) for offset, part in zip(chips, parts))]

    def own_swaps(q):
        own = lax.dynamic_index_in_dim(gathered[q], panel, 0, False)
        return [to_row(own, side) for side in range(1, group_count)]

    def cores(held, own_swapped):
        parts = list(held)
        for side in range(1, group_count):
            parts += [own_swapped[side - 1], *(to_row(h, side) for h in held[1:])]
        return parts

    held = in_plane(0, pieces(0))
    own_swapped = own_swaps(0)

    tag_parts = [part[-1, :rows_here, :panel_slots] for part in b_parts[1]]
    columns = jnp.stack(tag_parts).reshape(n_row, rows_here, group_count, slot_count)
    group_columns = lax.dynamic_index_in_dim(columns, group, 2, False)
    a_cols = group_columns
    for hop in range(1, n_col):
        pairs = [((r, r // group_count), (r, (r // group_count + hop) % n_col)) for r in range(n_row)]
        a_cols = jnp.where((col - panel) % n_col == hop, send(group_columns, pairs), a_cols)
    a_cols, *arrived = after(a_cols, *own_swapped, *held)
    own_swapped, held = arrived[: group_count - 1], arrived[group_count - 1 :]
    a_cols, b_cols = a_cols.astype(jnp.int32), columns.astype(jnp.int32)
    b_cols = b_cols + width_g * lax.broadcasted_iota(jnp.int32, columns.shape, 2)
    b_cols = b_cols.reshape(n_row, rows_here, panel_slots)
    onehot = a_cols[..., None] == jnp.arange(width_g, dtype=jnp.int32)
    wanted = jnp.sum(jnp.where(onehot[..., None], kept_columns, 0), axis=3)
    match = wanted[..., None] == b_cols[:, :, None, None, :]
    hit = jnp.max(jnp.where(match, jnp.arange(panel_slots, dtype=jnp.int32), -1), axis=-1)
    result = a_cols[..., None] * keep_count + jnp.arange(keep_count, dtype=jnp.int32)
    place = jnp.stack([(panel == col).astype(jnp.int32), group, panel]).astype(jnp.int32)
    codes = []
    for i, j in zip(cuts, cuts[1:]):
        rows_q = jnp.arange(n_row * (j - i), dtype=jnp.int32).reshape(n_row, j - i, 1, 1)
        code = (rows_q * panel_slots + hit[:, i:j]) * (1 << SHIFT) + result[:, i:j]
        codes.append(jnp.where(hit[:, i:j] >= 0, code, -1).reshape(-1))

    out, parts = None, pieces(1)
    for q in range(len(gathered)):
        a_parts = cores(held, own_swapped)
        if q + 1 < len(gathered):
            arrived = after(*parts, *held[1:])
            held[1:] = arrived[len(chips) :]
            coming = in_plane(q + 1, arrived[: len(chips)])
            own_swapped = own_swaps(q + 1)
        out = add_products(
            cuts[q : q + 2], codes[q], place, a_parts, [*b_parts[0], *b_parts[1]], out, out_blocks, group_count, slot_count
        )
        parts = []
        if q + 2 < len(gathered):
            out, gathered[q + 2] = after(out, gathered[q + 2])
            parts = pieces(q + 2)
        if q + 1 < len(gathered):
            out, *arrived = after(out, *own_swapped, *parts, *coming[1:])
            own_swapped, arrived = arrived[: group_count - 1], arrived[group_count - 1 :]
            parts, held = arrived[: len(parts)], [coming[0], *arrived[len(parts) :]]
    return out.reshape(width_g, keep_count, block_size, block_size)


def solution(mesh):
    placed = (P("row", "col", None, None, None), P("row", "col", None), P("row", "col"))
    return jax.shard_map(
        on_device,
        mesh=mesh,
        in_specs=placed,
        out_specs=P("row", "col", None, None),
        check_vma=False,
    )
```

```python
import functools

import jax
import jax.numpy as jnp
from jax import lax
from jax.experimental import pallas as pl
from jax.experimental.pallas import tpu as pltpu
from jax.sharding import PartitionSpec as P

SHIFT = 16
UNROLL = 8


def fill_plan(code_ref, plan_ref, seen, own, group, slot_count, group_count, keep_count, block_total):
    panel_slots = group_count * slot_count
    pairs = code_ref.shape[0]
    size = pairs + UNROLL
    b_base = pairs // keep_count

    def clear(block, carry):
        seen[block] = 0
        return carry

    lax.fori_loop(0, block_total, clear, 0)

    def note(at, counts):
        count, touched_count = counts
        row, slot = at // slot_count, at % slot_count
        a_at = jnp.where(own == 1, b_base + row * panel_slots + group * slot_count + slot, at)
        for keep in range(keep_count):
            code = code_ref[at * keep_count + keep]
            block = lax.bitwise_and(code, (1 << SHIFT) - 1)
            known = jnp.minimum(block, block_total - 1)
            plan_ref[2 + count] = a_at
            plan_ref[2 + size + count] = lax.shift_right_logical(code, SHIFT) + b_base
            plan_ref[2 + 2 * size + count] = block
            count = count + (code >= 0).astype(jnp.int32)
            fresh = jnp.logical_and(code >= 0, seen[known] == 0)
            plan_ref[2 + 3 * size + touched_count] = known
            seen[known] = jnp.where(code >= 0, 1, seen[known])
            touched_count = touched_count + fresh.astype(jnp.int32)
        return count, touched_count

    count, touched_count = lax.fori_loop(0, b_base, note, (jnp.int32(0), jnp.int32(0)))
    for k in range(UNROLL):
        plan_ref[2 + count + k] = b_base
        plan_ref[2 + size + count + k] = b_base
        plan_ref[2 + 2 * size + count + k] = block_total
    plan_ref[0] = (count + UNROLL - 1) // UNROLL
    plan_ref[1] = touched_count


def plan_kernel(place_ref, *refs, **sizes):
    chunk_count = len(refs) // 2
    for chunk in range(chunk_count):
        fill_plan(refs[chunk], refs[chunk_count + chunk], refs[-1], place_ref[0], place_ref[1], **sizes)


def plan_size(pairs, out_blocks):
    return 3 * (pairs + UNROLL) + out_blocks + 4


def make_plans(codes, place, out_blocks, group_count, slot_count, keep_count):
    scalars = pl.BlockSpec(memory_space=pltpu.SMEM)
    return pl.pallas_call(
        functools.partial(
            plan_kernel,
            slot_count=slot_count,
            group_count=group_count,
            keep_count=keep_count,
            block_total=out_blocks,
        ),
        out_shape=[jax.ShapeDtypeStruct((plan_size(code.shape[0], out_blocks),), jnp.int32) for code in codes],
        in_specs=[scalars] * (1 + len(codes)),
        out_specs=[scalars] * len(codes),
        scratch_shapes=[pltpu.SMEM((out_blocks,), jnp.int32)],
        cost_estimate=pl.CostEstimate(flops=0, bytes_accessed=1 << 10, transcendentals=0),
    )(place, *codes)


def product_kernel(plan_ref, place_ref, *refs, cuts, pairs, source_count, slot_count, group_count, first):
    chip_count, panel_slots = source_count // group_count, group_count * slot_count
    row0, row_count, pieces = cuts[0], cuts[-1] - cuts[0], list(zip(cuts, cuts[1:]))
    a_refs = []
    for _ in pieces:
        a_refs.append(refs[:source_count])
        refs = refs[source_count:]
    b_refs, refs = (refs[:source_count], refs[source_count : 2 * source_count]), refs[2 * source_count :]
    if not first:
        before_ref, refs = refs[0], refs[1:]
    own, group, panel = place_ref[0], place_ref[1], place_ref[2]
    size = pairs + UNROLL
    if first:
        code_ref, plan_ref, seen, refs = plan_ref, refs[-2], refs[-1], refs[:-2]
    out_ref, blocks, total, a_sem, b_sem, out_sem = refs
    a_size, b_size = row_count * slot_count, row_count * panel_slots
    b_base = source_count * a_size

    def a_part(source):
        return blocks.at[pl.ds(source * a_size, a_size)]

    def start_a(source):
        chip, side = source // group_count, source % group_count
        for piece, (i, j) in enumerate(pieces):
            at = source * a_size + (i - row0) * slot_count
            for row in range(j - i):
                held = a_refs[piece][side * chip_count + chip]
                held = held.at[panel] if len(held.shape) == 4 else held
                sent = held.at[pl.ds(row * panel_slots + group * slot_count, slot_count)]
                part = blocks.at[pl.ds(at + row * slot_count, slot_count)]
                pltpu.make_async_copy(sent, part, a_sem.at[source]).start()

    def wait_a(source):
        pltpu.make_async_copy(a_part(source), a_part(source), a_sem.at[source]).wait()

    half = b_refs[0][0].shape[0]
    b_start, b_end = row0 * panel_slots, (row0 + row_count) * panel_slots

    def b_copies(source):
        for at, (i, j) in enumerate(((b_start, min(b_end, half)), (max(b_start, half), b_end))):
            if i < j:
                sent = b_refs[at][source].at[pl.ds(i - at * half, j - i)]
                part = blocks.at[pl.ds(b_base + source * b_size + i - b_start, j - i)]
                yield pltpu.make_async_copy(sent, part, b_sem.at[at, source])

    def load(block):
        return pltpu.make_async_copy(before_ref.at[block], total.at[block], out_sem.at[block])

    def store(block):
        return pltpu.make_async_copy(total.at[block], out_ref.at[block], out_sem.at[block])

    for source in range(source_count):
        for copy in b_copies(source):
            copy.start()

    @pl.when(own == 0)
    def _():
        for source in range(source_count):
            start_a(source)

    def each_touched(act):
        def step(at, carry):
            act(plan_ref[2 + 3 * size + at])
            return carry

        lax.fori_loop(0, plan_ref[1], step, 0)

    if first:
        total[...] = jnp.zeros_like(total)
        keep_count = pairs // (source_count * row_count * slot_count)
        fill_plan(code_ref, plan_ref, seen, own, group, slot_count, group_count, keep_count, out_ref.shape[0])
    else:
        each_touched(lambda block: load(block).start())

    for source in range(source_count):
        for copy in b_copies(source):
            copy.wait()

    @pl.when(own == 0)
    def _():
        for source in range(source_count):
            wait_a(source)

    if not first:
        each_touched(lambda block: load(block).wait())

    def product(at):
        a, b = blocks[plan_ref[2 + at]], blocks[plan_ref[2 + size + at]]
        return lax.dot_general(a, b, (((0,), (0,)), ((), ())), preferred_element_type=jnp.float32)

    def several(step, carry):
        at = step * UNROLL
        values = [product(at + k) for k in range(UNROLL)]
        for k in range(UNROLL):
            total[plan_ref[2 + 2 * size + at + k]] += values[k]
        return carry

    lax.fori_loop(0, plan_ref[0], several, 0)
    if first:
        whole_store = pltpu.make_async_copy(total.at[pl.ds(0, out_ref.shape[0])], out_ref, out_sem.at[0])
        whole_store.start()
        whole_store.wait()
    else:
        each_touched(lambda block: store(block).start())
        each_touched(lambda block: store(block).wait())


def add_products(cuts, pairs, plan, place, a_parts, b_parts, before, out_blocks, group_count, slot_count):
    source_count, block_size, row_count = len(b_parts) // 2, b_parts[0].shape[-1], cuts[-1] - cuts[0]
    first = before is None
    anywhere = pl.BlockSpec(memory_space=pl.ANY)
    scalars = pl.BlockSpec(memory_space=pltpu.SMEM)
    operands = [plan, place, *a_parts, *b_parts] + ([] if first else [before])
    block_count = source_count * row_count * (1 + group_count) * slot_count
    return pl.pallas_call(
        functools.partial(
            product_kernel,
            cuts=cuts,
            pairs=pairs,
            source_count=source_count,
            slot_count=slot_count,
            group_count=group_count,
            first=first,
        ),
        out_shape=jax.ShapeDtypeStruct((out_blocks, block_size, block_size), jnp.float32),
        in_specs=[scalars, scalars] + [anywhere] * (len(operands) - 2),
        out_specs=anywhere,
        scratch_shapes=[
            pltpu.VMEM((block_count, block_size, block_size), jnp.bfloat16),
            pltpu.VMEM((out_blocks + 1, block_size, block_size), jnp.float32),
            pltpu.SemaphoreType.DMA((source_count,)),
            pltpu.SemaphoreType.DMA((2, source_count)),
            pltpu.SemaphoreType.DMA((out_blocks,)),
        ]
        + first
        * [pltpu.SMEM((plan_size(pairs, out_blocks),), jnp.int32), pltpu.SMEM((out_blocks,), jnp.int32)],
        input_output_aliases={} if first else {len(operands) - 1: 0},
        compiler_params=pltpu.CompilerParams(vmem_limit_bytes=52 << 20),
        cost_estimate=pl.CostEstimate(
            flops=2 * pairs * block_size**3,
            bytes_accessed=2 * block_count * block_size**2 + 8 * out_blocks * block_size**2,
            transcendentals=0,
        ),
    )(*operands)


def after(value, *others):
    return lax.optimization_barrier((value, *others))


def on_device(x_blocks, x_columns, kept_columns):
    rows_here, group_count, slot_count, block_size, _ = x_blocks.shape
    width_g, keep_count = kept_columns.shape
    n_row = lax.axis_size("row")
    n_col = lax.axis_size("col")
    row, col = lax.axis_index("row"), lax.axis_index("col")
    panel, group = row // group_count, row % group_count
    out_blocks = width_g * keep_count
    panel_slots = group_count * slot_count
    cuts = (0, rows_here * 8 // 16, rows_here * 13 // 16, rows_here)
    everyone = [(r, c) for r in range(n_row) for c in range(n_col)]

    def send(value, pairs):
        places = [(r * n_col + c, r2 * n_col + c2) for (r, c), (r2, c2) in pairs]
        return lax.ppermute(value, ("row", "col"), places)

    def to_row(value, offset, skip_panel=False):
        return send(
            value,
            [
                ((r, c), (r ^ offset, c))
                for r, c in everyone
                if not (skip_panel and (r ^ offset) // group_count == c)
            ],
        )

    x_flat = x_blocks.reshape(rows_here * panel_slots, block_size, block_size)
    first_part = x_flat[: cuts[1] * panel_slots]
    x_rest, first_part = after(x_flat, first_part)
    gathered = [lax.all_gather(first_part, "col")]
    for i, j in zip(cuts[1:], cuts[2:]):
        gathered.append(lax.all_gather(x_rest[i * panel_slots : j * panel_slots], "col"))
    tags = x_columns.reshape(rows_here, panel_slots).astype(jnp.bfloat16)
    tags = jnp.pad(tags, ((0, block_size - rows_here), (0, block_size - panel_slots)))
    half = rows_here * panel_slots // 2
    halves = [
        first_part if half == cuts[1] * panel_slots else x_flat[:half],
        jnp.concatenate([x_rest[half:], tags[None]]),
    ]

    chips = range(group_count, n_row, group_count)
    near = [offset for offset in chips if not (offset // group_count) & (offset // group_count - 1)]
    far = [offset for offset in chips if offset not in near]
    b_parts = [[part] + [None] * (n_row - 1) for part in halves]
    for at in range(2):
        for offset in near if at else near[::-1]:
            b_parts[at][offset] = to_row(halves[at], offset)
    for offset in sorted(far, key=lambda offset: bin(offset).count("1")):
        steps = [step for step in near if step & offset]
        for at, step in enumerate((steps[0], steps[-1])):
            b_parts[at][offset] = to_row(b_parts[at][offset ^ step], step)
    for at in range(2):
        for offset in (0, *near):
            for side in range(1, group_count):
                b_parts[at][offset + side] = to_row(b_parts[at][offset], side)
    there = [(at, offset) for at in range(2) for offset in range(n_row) if b_parts[at][offset] is not None]
    gathered[0], *arrived = after(gathered[0], *(b_parts[at][offset] for at, offset in there))
    for (at, offset), part in zip(there, arrived):
        b_parts[at][offset] = part
    for at in range(2):
        for offset in far:
            for side in range(1, group_count):
                b_parts[at][offset + side] = to_row(b_parts[at][offset], side)

    def pieces(q):
        return [
            lax.dynamic_index_in_dim(gathered[q], panel ^ (offset // group_count), 0, False) for offset in chips
        ]

    def in_plane(q, parts):
        return [gathered[q], *(to_row(part, offset, True) for offset, part in zip(chips, parts))]

    def own_swaps(q):
        own = lax.dynamic_index_in_dim(gathered[q], panel, 0, False)
        return [to_row(own, side) for side in range(1, group_count)]

    def cores(held, own_swapped):
        parts = list(held)
        for side in range(1, group_count):
            parts += [own_swapped[side - 1], *(to_row(h, side) for h in held[1:])]
        return parts

    held = in_plane(0, pieces(0))
    own_swapped = own_swaps(0)

    tag_parts = [part[-1, :rows_here, :panel_slots] for part in b_parts[1]]
    columns = jnp.stack(tag_parts).reshape(n_row, rows_here, group_count, slot_count)
    group_columns = lax.dynamic_index_in_dim(columns, group, 2, False)
    a_cols = group_columns
    for hop in range(1, n_col):
        pairs = [((r, r // group_count), (r, (r // group_count + hop) % n_col)) for r in range(n_row)]
        a_cols = jnp.where((col - panel) % n_col == hop, send(group_columns, pairs), a_cols)
    a_cols, *arrived = after(a_cols, *own_swapped, *held)
    own_swapped, held = arrived[: group_count - 1], arrived[group_count - 1 :]
    a_cols, b_cols = a_cols.astype(jnp.int32), columns.astype(jnp.int32)
    b_cols = b_cols + width_g * lax.broadcasted_iota(jnp.int32, columns.shape, 2)
    b_cols = b_cols.reshape(n_row, rows_here, panel_slots)
    onehot = a_cols[..., None] == jnp.arange(width_g, dtype=jnp.int32)
    wanted = jnp.sum(jnp.where(onehot[..., None], kept_columns, 0), axis=3)
    match = wanted[..., None] == b_cols[:, :, None, None, :]
    hit = jnp.max(jnp.where(match, jnp.arange(panel_slots, dtype=jnp.int32), -1), axis=-1)
    result = a_cols[..., None] * keep_count + jnp.arange(keep_count, dtype=jnp.int32)
    place = jnp.stack([(panel == col).astype(jnp.int32), group, panel]).astype(jnp.int32)
    codes = []
    for i, j in zip(cuts, cuts[1:]):
        rows_q = jnp.arange(n_row * (j - i), dtype=jnp.int32).reshape(n_row, j - i, 1, 1)
        code = (rows_q * panel_slots + hit[:, i:j]) * (1 << SHIFT) + result[:, i:j]
        codes.append(jnp.where(hit[:, i:j] >= 0, code, -1).reshape(-1))

    out, parts, plans = None, pieces(1), codes[:1]
    for q in range(len(gathered)):
        a_parts = cores(held, own_swapped)
        if q + 1 < len(gathered):
            arrived = after(*parts, *held[1:])
            held[1:] = arrived[len(chips) :]
            coming = in_plane(q + 1, arrived[: len(chips)])
            own_swapped = own_swaps(q + 1)
        out = add_products(
            cuts[q : q + 2], codes[q].shape[0], plans[q], place, a_parts, [*b_parts[0], *b_parts[1]], out, out_blocks, group_count, slot_count
        )
        parts = []
        if q + 2 < len(gathered):
            if q == 0:
                out, *later = after(out, *codes[1:])
                plans += make_plans(later, place, out_blocks, group_count, slot_count, keep_count)
            out, gathered[q + 2], *plans = after(out, gathered[q + 2], *plans)
            parts = pieces(q + 2)
        if q + 1 < len(gathered):
            out, *arrived = after(out, *own_swapped, *parts, *coming[1:])
            own_swapped, arrived = arrived[: group_count - 1], arrived[group_count - 1 :]
            parts, held = arrived[: len(parts)], [coming[0], *arrived[len(parts) :]]
    return out.reshape(width_g, keep_count, block_size, block_size)


def solution(mesh):
    placed = (P("row", "col", None, None, None), P("row", "col", None), P("row", "col"))
    return jax.shard_map(
        on_device,
        mesh=mesh,
        in_specs=placed,
        out_specs=P("row", "col", None, None),
        check_vma=False,
    )
```

```python
import functools

import jax
import jax.numpy as jnp
from jax import lax
from jax.experimental import pallas as pl
from jax.experimental.pallas import tpu as pltpu
from jax.sharding import PartitionSpec as P

SHIFT = 16
UNROLL = 8


def fill_plan(code_ref, plan_ref, seen, own, group, slot_count, group_count, keep_count, block_total):
    panel_slots = group_count * slot_count
    pairs = code_ref.shape[0]
    size = pairs + UNROLL
    b_base = pairs // keep_count

    def clear(block, carry):
        seen[block] = 0
        return carry

    lax.fori_loop(0, block_total, clear, 0)

    def note(at, counts):
        count, touched_count = counts
        row, slot = at // slot_count, at % slot_count
        a_at = jnp.where(own == 1, b_base + row * panel_slots + group * slot_count + slot, at)
        for keep in range(keep_count):
            code = code_ref[at * keep_count + keep]
            block = lax.bitwise_and(code, (1 << SHIFT) - 1)
            known = jnp.minimum(block, block_total - 1)
            plan_ref[2 + count] = a_at
            plan_ref[2 + size + count] = lax.shift_right_logical(code, SHIFT) + b_base
            plan_ref[2 + 2 * size + count] = block
            count = count + (code >= 0).astype(jnp.int32)
            fresh = jnp.logical_and(code >= 0, seen[known] == 0)
            plan_ref[2 + 3 * size + touched_count] = known
            seen[known] = jnp.where(code >= 0, 1, seen[known])
            touched_count = touched_count + fresh.astype(jnp.int32)
        return count, touched_count

    count, touched_count = lax.fori_loop(0, b_base, note, (jnp.int32(0), jnp.int32(0)))
    for k in range(UNROLL):
        plan_ref[2 + count + k] = b_base
        plan_ref[2 + size + count + k] = b_base
        plan_ref[2 + 2 * size + count + k] = block_total
    plan_ref[0] = (count + UNROLL - 1) // UNROLL
    plan_ref[1] = touched_count


def plan_kernel(place_ref, *refs, **sizes):
    chunk_count = len(refs) // 2
    for chunk in range(chunk_count):
        fill_plan(refs[chunk], refs[chunk_count + chunk], refs[-1], place_ref[0], place_ref[1], **sizes)


def plan_size(pairs, out_blocks):
    return 3 * (pairs + UNROLL) + out_blocks + 4


def make_plans(codes, place, out_blocks, group_count, slot_count, keep_count):
    scalars = pl.BlockSpec(memory_space=pltpu.SMEM)
    return pl.pallas_call(
        functools.partial(
            plan_kernel,
            slot_count=slot_count,
            group_count=group_count,
            keep_count=keep_count,
            block_total=out_blocks,
        ),
        out_shape=[jax.ShapeDtypeStruct((plan_size(code.shape[0], out_blocks),), jnp.int32) for code in codes],
        in_specs=[scalars] * (1 + len(codes)),
        out_specs=[scalars] * len(codes),
        scratch_shapes=[pltpu.SMEM((out_blocks,), jnp.int32)],
        cost_estimate=pl.CostEstimate(flops=0, bytes_accessed=1 << 10, transcendentals=0),
    )(place, *codes)


def product_kernel(plan_ref, place_ref, *refs, cuts, pairs, source_count, slot_count, group_count, first):
    chip_count, panel_slots = source_count // group_count, group_count * slot_count
    row0, row_count, pieces = cuts[0], cuts[-1] - cuts[0], list(zip(cuts, cuts[1:]))
    a_refs = []
    for _ in pieces:
        a_refs.append(refs[:source_count])
        refs = refs[source_count:]
    b_refs, refs = (refs[:source_count], refs[source_count : 2 * source_count]), refs[2 * source_count :]
    if not first:
        before_ref, refs = refs[0], refs[1:]
    own, group, panel = place_ref[0], place_ref[1], place_ref[2]
    size = pairs + UNROLL
    if first:
        code_ref, plan_ref, seen, refs = plan_ref, refs[-2], refs[-1], refs[:-2]
    out_ref, blocks, total, a_sem, b_sem, out_sem = refs
    a_size, b_size = row_count * slot_count, row_count * panel_slots
    b_base = source_count * a_size

    def a_part(source):
        return blocks.at[pl.ds(source * a_size, a_size)]

    def start_a(source):
        chip, side = source // group_count, source % group_count
        for piece, (i, j) in enumerate(pieces):
            at = source * a_size + (i - row0) * slot_count
            for row in range(j - i):
                held = a_refs[piece][side * chip_count + chip]
                held = held.at[panel] if len(held.shape) == 4 else held
                sent = held.at[pl.ds(row * panel_slots + group * slot_count, slot_count)]
                part = blocks.at[pl.ds(at + row * slot_count, slot_count)]
                pltpu.make_async_copy(sent, part, a_sem.at[source]).start()

    def wait_a(source):
        pltpu.make_async_copy(a_part(source), a_part(source), a_sem.at[source]).wait()

    half = b_refs[0][0].shape[0]
    b_start, b_end = row0 * panel_slots, (row0 + row_count) * panel_slots

    def b_copies(source):
        for at, (i, j) in enumerate(((b_start, min(b_end, half)), (max(b_start, half), b_end))):
            if i < j:
                sent = b_refs[at][source].at[pl.ds(i - at * half, j - i)]
                part = blocks.at[pl.ds(b_base + source * b_size + i - b_start, j - i)]
                yield pltpu.make_async_copy(sent, part, b_sem.at[at, source])

    def load(block):
        return pltpu.make_async_copy(before_ref.at[block], total.at[block], out_sem.at[block])

    def store(block):
        return pltpu.make_async_copy(total.at[block], out_ref.at[block], out_sem.at[block])

    for source in range(source_count):
        for copy in b_copies(source):
            copy.start()

    @pl.when(own == 0)
    def _():
        for source in range(source_count):
            start_a(source)

    def each_touched(act):
        def step(at, carry):
            act(plan_ref[2 + 3 * size + at])
            return carry

        lax.fori_loop(0, plan_ref[1], step, 0)

    if first:
        total[...] = jnp.zeros_like(total)
        keep_count = pairs // (source_count * row_count * slot_count)
        fill_plan(code_ref, plan_ref, seen, own, group, slot_count, group_count, keep_count, out_ref.shape[0])
    else:
        each_touched(lambda block: load(block).start())

    for source in range(source_count):
        for copy in b_copies(source):
            copy.wait()

    @pl.when(own == 0)
    def _():
        for source in range(source_count):
            wait_a(source)

    if not first:
        each_touched(lambda block: load(block).wait())

    def product(at):
        a, b = blocks[plan_ref[2 + at]], blocks[plan_ref[2 + size + at]]
        return lax.dot_general(a, b, (((0,), (0,)), ((), ())), preferred_element_type=jnp.float32)

    def several(step, carry):
        at = step * UNROLL
        values = [product(at + k) for k in range(UNROLL)]
        for k in range(UNROLL):
            total[plan_ref[2 + 2 * size + at + k]] += values[k]
        return carry

    lax.fori_loop(0, plan_ref[0], several, 0)
    if first:
        whole_store = pltpu.make_async_copy(total.at[pl.ds(0, out_ref.shape[0])], out_ref, out_sem.at[0])
        whole_store.start()
        whole_store.wait()
    else:
        each_touched(lambda block: store(block).start())
        each_touched(lambda block: store(block).wait())


def add_products(cuts, pairs, plan, place, a_parts, b_parts, before, out_blocks, group_count, slot_count):
    source_count, block_size, row_count = len(b_parts) // 2, b_parts[0].shape[-1], cuts[-1] - cuts[0]
    first = before is None
    anywhere = pl.BlockSpec(memory_space=pl.ANY)
    scalars = pl.BlockSpec(memory_space=pltpu.SMEM)
    operands = [plan, place, *a_parts, *b_parts] + ([] if first else [before])
    block_count = source_count * row_count * (1 + group_count) * slot_count
    return pl.pallas_call(
        functools.partial(
            product_kernel,
            cuts=cuts,
            pairs=pairs,
            source_count=source_count,
            slot_count=slot_count,
            group_count=group_count,
            first=first,
        ),
        out_shape=jax.ShapeDtypeStruct((out_blocks, block_size, block_size), jnp.float32),
        in_specs=[scalars, scalars] + [anywhere] * (len(operands) - 2),
        out_specs=anywhere,
        scratch_shapes=[
            pltpu.VMEM((block_count, block_size, block_size), jnp.bfloat16),
            pltpu.VMEM((out_blocks + 1, block_size, block_size), jnp.float32),
            pltpu.SemaphoreType.DMA((source_count,)),
            pltpu.SemaphoreType.DMA((2, source_count)),
            pltpu.SemaphoreType.DMA((out_blocks,)),
        ]
        + first
        * [pltpu.SMEM((plan_size(pairs, out_blocks),), jnp.int32), pltpu.SMEM((out_blocks,), jnp.int32)],
        input_output_aliases={} if first else {len(operands) - 1: 0},
        compiler_params=pltpu.CompilerParams(vmem_limit_bytes=52 << 20),
        cost_estimate=pl.CostEstimate(
            flops=2 * pairs * block_size**3,
            bytes_accessed=2 * block_count * block_size**2 + 8 * out_blocks * block_size**2,
            transcendentals=0,
        ),
    )(*operands)


def after(value, *others):
    return lax.optimization_barrier((value, *others))


def on_device(x_blocks, x_columns, kept_columns):
    rows_here, group_count, slot_count, block_size, _ = x_blocks.shape
    width_g, keep_count = kept_columns.shape
    n_row = lax.axis_size("row")
    n_col = lax.axis_size("col")
    row, col = lax.axis_index("row"), lax.axis_index("col")
    panel, group = row // group_count, row % group_count
    out_blocks = width_g * keep_count
    panel_slots = group_count * slot_count
    cuts = (0, rows_here * 8 // 16, rows_here * 13 // 16, rows_here)
    everyone = [(r, c) for r in range(n_row) for c in range(n_col)]

    def send(value, pairs):
        places = [(r * n_col + c, r2 * n_col + c2) for (r, c), (r2, c2) in pairs]
        return lax.ppermute(value, ("row", "col"), places)

    def to_row(value, offset, skip_panel=False):
        return send(
            value,
            [
                ((r, c), (r ^ offset, c))
                for r, c in everyone
                if not (skip_panel and (r ^ offset) // group_count == c)
            ],
        )

    x_flat = x_blocks.reshape(rows_here * panel_slots, block_size, block_size)
    first_part = x_flat[: cuts[1] * panel_slots]
    x_rest, first_part = after(x_flat, first_part)
    gathered = [lax.all_gather(first_part, "col")]
    for i, j in zip(cuts[1:], cuts[2:]):
        gathered.append(lax.all_gather(x_rest[i * panel_slots : j * panel_slots], "col"))
    tags = x_columns.reshape(rows_here, panel_slots).astype(jnp.bfloat16)
    tags = jnp.pad(tags, ((0, block_size - rows_here), (0, block_size - panel_slots)))
    half = rows_here * panel_slots // 2
    halves = [
        first_part if half == cuts[1] * panel_slots else x_flat[:half],
        jnp.concatenate([x_rest[half:], tags[None]]),
    ]

    chips = range(group_count, n_row, group_count)
    near = [offset for offset in chips if not (offset // group_count) & (offset // group_count - 1)]
    far = [offset for offset in chips if offset not in near]
    b_parts = [[part] + [None] * (n_row - 1) for part in halves]
    for at in range(2):
        for offset in near if at else near[::-1]:
            b_parts[at][offset] = to_row(halves[at], offset)
    for offset in sorted(far, key=lambda offset: bin(offset).count("1")):
        steps = [step for step in near if step & offset]
        for at, step in enumerate((steps[0], steps[-1])):
            b_parts[at][offset] = to_row(b_parts[at][offset ^ step], step)
    for at in range(2):
        for offset in (0, *near):
            for side in range(1, group_count):
                b_parts[at][offset + side] = to_row(b_parts[at][offset], side)
    there = [(at, offset) for at in range(2) for offset in range(n_row) if b_parts[at][offset] is not None]
    gathered[0], *arrived = after(gathered[0], *(b_parts[at][offset] for at, offset in there))
    for (at, offset), part in zip(there, arrived):
        b_parts[at][offset] = part
    for at in range(2):
        for offset in far:
            for side in range(1, group_count):
                b_parts[at][offset + side] = to_row(b_parts[at][offset], side)

    def pieces(q):
        return [
            lax.dynamic_index_in_dim(gathered[q], panel ^ (offset // group_count), 0, False) for offset in chips
        ]

    def in_plane(q, parts):
        return [gathered[q], *(to_row(part, offset, True) for offset, part in zip(chips, parts))]

    def own_swaps(q):
        own = lax.dynamic_index_in_dim(gathered[q], panel, 0, False)
        return [to_row(own, side) for side in range(1, group_count)]

    def cores(held, own_swapped):
        parts = list(held)
        for side in range(1, group_count):
            parts += [own_swapped[side - 1], *(to_row(h, side) for h in held[1:])]
        return parts

    held = in_plane(0, pieces(0))
    own_swapped = own_swaps(0)

    tag_parts = [part[-1, :rows_here, :panel_slots] for part in b_parts[1]]
    columns = jnp.stack(tag_parts).reshape(n_row, rows_here, group_count, slot_count)
    group_columns = lax.dynamic_index_in_dim(columns, group, 2, False)
    a_cols = group_columns
    for hop in range(1, n_col):
        pairs = [((r, r // group_count), (r, (r // group_count + hop) % n_col)) for r in range(n_row)]
        a_cols = jnp.where((col - panel) % n_col == hop, send(group_columns, pairs), a_cols)
    a_cols, gathered[1], *arrived = after(a_cols, gathered[1], *own_swapped, *held)
    own_swapped, held = arrived[: group_count - 1], arrived[group_count - 1 :]
    a_cols, b_cols = a_cols.astype(jnp.int32), columns.astype(jnp.int32)
    b_cols = b_cols + width_g * lax.broadcasted_iota(jnp.int32, columns.shape, 2)
    b_cols = b_cols.reshape(n_row, rows_here, panel_slots)
    onehot = a_cols[..., None] == jnp.arange(width_g, dtype=jnp.int32)
    wanted = jnp.sum(jnp.where(onehot[..., None], kept_columns, 0), axis=3)
    match = wanted[..., None] == b_cols[:, :, None, None, :]
    hit = jnp.max(jnp.where(match, jnp.arange(panel_slots, dtype=jnp.int32), -1), axis=-1)
    result = a_cols[..., None] * keep_count + jnp.arange(keep_count, dtype=jnp.int32)
    place = jnp.stack([(panel == col).astype(jnp.int32), group, panel]).astype(jnp.int32)
    codes = []
    for i, j in zip(cuts, cuts[1:]):
        rows_q = jnp.arange(n_row * (j - i), dtype=jnp.int32).reshape(n_row, j - i, 1, 1)
        code = (rows_q * panel_slots + hit[:, i:j]) * (1 << SHIFT) + result[:, i:j]
        codes.append(jnp.where(hit[:, i:j] >= 0, code, -1).reshape(-1))

    out, parts, plans = None, pieces(1), codes[:1]
    for q in range(len(gathered)):
        a_parts = cores(held, own_swapped)
        if q + 1 < len(gathered):
            arrived = after(*parts, *held[1:])
            held[1:] = arrived[len(chips) :]
            coming = in_plane(q + 1, arrived[: len(chips)])
            own_swapped = own_swaps(q + 1)
        out = add_products(
            cuts[q : q + 2], codes[q].shape[0], plans[q], place, a_parts, [*b_parts[0], *b_parts[1]], out, out_blocks, group_count, slot_count
        )
        parts = []
        if q + 2 < len(gathered):
            if q == 0:
                out, *later = after(out, *codes[1:])
                plans += make_plans(later, place, out_blocks, group_count, slot_count, keep_count)
            out, gathered[q + 2], *plans = after(out, gathered[q + 2], *plans)
            parts = pieces(q + 2)
        if q + 1 < len(gathered):
            out, *arrived = after(out, *own_swapped, *parts, *coming[1:])
            own_swapped, arrived = arrived[: group_count - 1], arrived[group_count - 1 :]
            parts, held = arrived[: len(parts)], [coming[0], *arrived[len(parts) :]]
    return out.reshape(width_g, keep_count, block_size, block_size)


def solution(mesh):
    placed = (P("row", "col", None, None, None), P("row", "col", None), P("row", "col"))
    return jax.shard_map(
        on_device,
        mesh=mesh,
        in_specs=placed,
        out_specs=P("row", "col", None, None),
        check_vma=False,
    )
```

```python
import functools

import jax
import jax.numpy as jnp
from jax import lax
from jax.experimental import pallas as pl
from jax.experimental.pallas import tpu as pltpu
from jax.sharding import PartitionSpec as P

SHIFT = 16
UNROLL = 8


def fill_plan(
    code_ref, plan_ref, seen, own, group, slot_count, group_count, keep_count, block_total, with_touched=True
):
    panel_slots = group_count * slot_count
    pairs = code_ref.shape[0]
    size = pairs + UNROLL
    b_base = pairs // keep_count

    def clear(block, carry):
        seen[block] = 0
        return carry

    if with_touched:
        lax.fori_loop(0, block_total, clear, 0)

    def note(at, counts):
        count, touched_count = counts
        row, slot = at // slot_count, at % slot_count
        a_at = jnp.where(own == 1, b_base + row * panel_slots + group * slot_count + slot, at)
        for keep in range(keep_count):
            code = code_ref[at * keep_count + keep]
            block = lax.bitwise_and(code, (1 << SHIFT) - 1)
            plan_ref[2 + count] = a_at
            plan_ref[2 + size + count] = lax.shift_right_logical(code, SHIFT) + b_base
            plan_ref[2 + 2 * size + count] = block
            count = count + (code >= 0).astype(jnp.int32)
            if with_touched:
                known = jnp.minimum(block, block_total - 1)
                fresh = jnp.logical_and(code >= 0, seen[known] == 0)
                plan_ref[2 + 3 * size + touched_count] = known
                seen[known] = jnp.where(code >= 0, 1, seen[known])
                touched_count = touched_count + fresh.astype(jnp.int32)
        return count, touched_count

    count, touched_count = lax.fori_loop(0, b_base, note, (jnp.int32(0), jnp.int32(0)))
    for k in range(UNROLL):
        plan_ref[2 + count + k] = b_base
        plan_ref[2 + size + count + k] = b_base
        plan_ref[2 + 2 * size + count + k] = block_total
    plan_ref[0] = (count + UNROLL - 1) // UNROLL
    plan_ref[1] = touched_count


def plan_kernel(place_ref, *refs, **sizes):
    chunk_count = len(refs) // 2
    for chunk in range(chunk_count):
        fill_plan(refs[chunk], refs[chunk_count + chunk], refs[-1], place_ref[0], place_ref[1], **sizes)


def plan_size(pairs, out_blocks):
    return 3 * (pairs + UNROLL) + out_blocks + 4


def make_plans(codes, place, out_blocks, group_count, slot_count, keep_count):
    scalars = pl.BlockSpec(memory_space=pltpu.SMEM)
    return pl.pallas_call(
        functools.partial(
            plan_kernel,
            slot_count=slot_count,
            group_count=group_count,
            keep_count=keep_count,
            block_total=out_blocks,
        ),
        out_shape=[jax.ShapeDtypeStruct((plan_size(code.shape[0], out_blocks),), jnp.int32) for code in codes],
        in_specs=[scalars] * (1 + len(codes)),
        out_specs=[scalars] * len(codes),
        scratch_shapes=[pltpu.SMEM((out_blocks,), jnp.int32)],
        cost_estimate=pl.CostEstimate(flops=0, bytes_accessed=1 << 10, transcendentals=0),
    )(place, *codes)


def product_kernel(plan_ref, place_ref, *refs, cuts, pairs, source_count, slot_count, group_count, first, planned):
    chip_count, panel_slots = source_count // group_count, group_count * slot_count
    row0, row_count, pieces = cuts[0], cuts[-1] - cuts[0], list(zip(cuts, cuts[1:]))
    a_refs = []
    for _ in pieces:
        a_refs.append(refs[:source_count])
        refs = refs[source_count:]
    b_refs, refs = (refs[:source_count], refs[source_count : 2 * source_count]), refs[2 * source_count :]
    if not first:
        before_ref, refs = refs[0], refs[1:]
    own, group, panel = place_ref[0], place_ref[1], place_ref[2]
    size = pairs + UNROLL
    if not planned:
        code_ref, plan_ref, seen, refs = plan_ref, refs[-2], refs[-1], refs[:-2]
    out_ref, blocks, total, a_sem, b_sem, out_sem = refs
    a_size, b_size = row_count * slot_count, row_count * panel_slots
    b_base = source_count * a_size

    def a_part(source):
        return blocks.at[pl.ds(source * a_size, a_size)]

    def start_a(source):
        chip, side = source // group_count, source % group_count
        for piece, (i, j) in enumerate(pieces):
            at = source * a_size + (i - row0) * slot_count
            for row in range(j - i):
                held = a_refs[piece][side * chip_count + chip]
                held = held.at[panel] if len(held.shape) == 4 else held
                sent = held.at[pl.ds(row * panel_slots + group * slot_count, slot_count)]
                part = blocks.at[pl.ds(at + row * slot_count, slot_count)]
                pltpu.make_async_copy(sent, part, a_sem.at[source]).start()

    def wait_a(source):
        pltpu.make_async_copy(a_part(source), a_part(source), a_sem.at[source]).wait()

    half = b_refs[0][0].shape[0]
    b_start, b_end = row0 * panel_slots, (row0 + row_count) * panel_slots

    def b_copies(source):
        for at, (i, j) in enumerate(((b_start, min(b_end, half)), (max(b_start, half), b_end))):
            if i < j:
                sent = b_refs[at][source].at[pl.ds(i - at * half, j - i)]
                part = blocks.at[pl.ds(b_base + source * b_size + i - b_start, j - i)]
                yield pltpu.make_async_copy(sent, part, b_sem.at[at, source])

    def load(block):
        return pltpu.make_async_copy(before_ref.at[block], total.at[block], out_sem.at[block])

    def store(block):
        return pltpu.make_async_copy(total.at[block], out_ref.at[block], out_sem.at[block])

    for source in range(source_count):
        for copy in b_copies(source):
            copy.start()

    @pl.when(own == 0)
    def _():
        for source in range(source_count):
            start_a(source)

    def each_touched(act):
        def step(at, carry):
            act(plan_ref[2 + 3 * size + at])
            return carry

        lax.fori_loop(0, plan_ref[1], step, 0)

    if first:
        total[...] = jnp.zeros_like(total)
    if not planned:
        keep_count = pairs // (source_count * row_count * slot_count)
        fill_plan(
            code_ref, plan_ref, seen, own, group, slot_count, group_count, keep_count, out_ref.shape[0], not first
        )
    if not first:
        each_touched(lambda block: load(block).start())

    for source in range(source_count):
        for copy in b_copies(source):
            copy.wait()

    @pl.when(own == 0)
    def _():
        for source in range(source_count):
            wait_a(source)

    if not first:
        each_touched(lambda block: load(block).wait())

    def product(at):
        a, b = blocks[plan_ref[2 + at]], blocks[plan_ref[2 + size + at]]
        return lax.dot_general(a, b, (((0,), (0,)), ((), ())), preferred_element_type=jnp.float32)

    def several(step, carry):
        at = step * UNROLL
        values = [product(at + k) for k in range(UNROLL)]
        for k in range(UNROLL):
            total[plan_ref[2 + 2 * size + at + k]] += values[k]
        return carry

    lax.fori_loop(0, plan_ref[0], several, 0)
    if first:
        whole_store = pltpu.make_async_copy(total.at[pl.ds(0, out_ref.shape[0])], out_ref, out_sem.at[0])
        whole_store.start()
        whole_store.wait()
    else:
        each_touched(lambda block: store(block).start())
        each_touched(lambda block: store(block).wait())


def add_products(cuts, pairs, plan, place, a_parts, b_parts, before, out_blocks, group_count, slot_count, planned):
    source_count, block_size, row_count = len(b_parts) // 2, b_parts[0].shape[-1], cuts[-1] - cuts[0]
    first = before is None
    anywhere = pl.BlockSpec(memory_space=pl.ANY)
    scalars = pl.BlockSpec(memory_space=pltpu.SMEM)
    operands = [plan, place, *a_parts, *b_parts] + ([] if first else [before])
    block_count = source_count * row_count * (1 + group_count) * slot_count
    return pl.pallas_call(
        functools.partial(
            product_kernel,
            cuts=cuts,
            pairs=pairs,
            source_count=source_count,
            slot_count=slot_count,
            group_count=group_count,
            first=first,
            planned=planned,
        ),
        out_shape=jax.ShapeDtypeStruct((out_blocks, block_size, block_size), jnp.float32),
        in_specs=[scalars, scalars] + [anywhere] * (len(operands) - 2),
        out_specs=anywhere,
        scratch_shapes=[
            pltpu.VMEM((block_count, block_size, block_size), jnp.bfloat16),
            pltpu.VMEM((out_blocks + 1, block_size, block_size), jnp.float32),
            pltpu.SemaphoreType.DMA((source_count,)),
            pltpu.SemaphoreType.DMA((2, source_count)),
            pltpu.SemaphoreType.DMA((out_blocks,)),
        ]
        + (not planned)
        * [pltpu.SMEM((plan_size(pairs, out_blocks),), jnp.int32), pltpu.SMEM((out_blocks,), jnp.int32)],
        input_output_aliases={} if first else {len(operands) - 1: 0},
        compiler_params=pltpu.CompilerParams(vmem_limit_bytes=52 << 20),
        cost_estimate=pl.CostEstimate(
            flops=2 * pairs * block_size**3,
            bytes_accessed=2 * block_count * block_size**2 + 8 * out_blocks * block_size**2,
            transcendentals=0,
        ),
    )(*operands)


def after(value, *others):
    return lax.optimization_barrier((value, *others))


def on_device(x_blocks, x_columns, kept_columns):
    rows_here, group_count, slot_count, block_size, _ = x_blocks.shape
    width_g, keep_count = kept_columns.shape
    n_row = lax.axis_size("row")
    n_col = lax.axis_size("col")
    row, col = lax.axis_index("row"), lax.axis_index("col")
    panel, group = row // group_count, row % group_count
    out_blocks = width_g * keep_count
    panel_slots = group_count * slot_count
    cuts = (0, rows_here * 8 // 16, rows_here * 13 // 16, rows_here)
    everyone = [(r, c) for r in range(n_row) for c in range(n_col)]

    def send(value, pairs):
        places = [(r * n_col + c, r2 * n_col + c2) for (r, c), (r2, c2) in pairs]
        return lax.ppermute(value, ("row", "col"), places)

    def to_row(value, offset, skip_panel=False):
        return send(
            value,
            [
                ((r, c), (r ^ offset, c))
                for r, c in everyone
                if not (skip_panel and (r ^ offset) // group_count == c)
            ],
        )

    x_flat = x_blocks.reshape(rows_here * panel_slots, block_size, block_size)
    first_part = x_flat[: cuts[1] * panel_slots]
    x_rest, first_part = after(x_flat, first_part)
    gathered = [lax.all_gather(first_part, "col")]
    operands = after(*(x_rest[i * panel_slots : j * panel_slots] for i, j in zip(cuts[1:], cuts[2:])))
    gathered += [lax.all_gather(operand, "col") for operand in operands]
    tags = x_columns.reshape(rows_here, panel_slots).astype(jnp.bfloat16)
    tags = jnp.pad(tags, ((0, block_size - rows_here), (0, block_size - panel_slots)))
    half = rows_here * panel_slots // 2
    halves = [
        first_part if half == cuts[1] * panel_slots else x_flat[:half],
        jnp.concatenate([x_rest[half:], tags[None]]),
    ]

    chips = range(group_count, n_row, group_count)
    near = [offset for offset in chips if not (offset // group_count) & (offset // group_count - 1)]
    far = [offset for offset in chips if offset not in near]
    b_parts = [[part] + [None] * (n_row - 1) for part in halves]
    for at in range(2):
        for offset in near if at else near[::-1]:
            b_parts[at][offset] = to_row(halves[at], offset)
    for offset in sorted(far, key=lambda offset: bin(offset).count("1")):
        steps = [step for step in near if step & offset]
        for at, step in enumerate((steps[0], steps[-1])):
            b_parts[at][offset] = to_row(b_parts[at][offset ^ step], step)
    for at in range(2):
        for offset in (0, *near):
            for side in range(1, group_count):
                b_parts[at][offset + side] = to_row(b_parts[at][offset], side)
    there = [(at, offset) for at in range(2) for offset in range(n_row) if b_parts[at][offset] is not None]
    gathered[0], *arrived = after(gathered[0], *(b_parts[at][offset] for at, offset in there))
    for (at, offset), part in zip(there, arrived):
        b_parts[at][offset] = part
    for at in range(2):
        for offset in far:
            for side in range(1, group_count):
                b_parts[at][offset + side] = to_row(b_parts[at][offset], side)

    def pieces(q):
        return [
            lax.dynamic_index_in_dim(gathered[q], panel ^ (offset // group_count), 0, False) for offset in chips
        ]

    def in_plane(q, parts):
        return [gathered[q], *(to_row(part, offset, True) for offset, part in zip(chips, parts))]

    def own_swaps(q):
        own = lax.dynamic_index_in_dim(gathered[q], panel, 0, False)
        return [to_row(own, side) for side in range(1, group_count)]

    def cores(held, own_swapped):
        parts = list(held)
        for side in range(1, group_count):
            parts += [own_swapped[side - 1], *(to_row(h, side) for h in held[1:])]
        return parts

    held = in_plane(0, pieces(0))
    own_swapped = own_swaps(0)

    tag_parts = [part[-1, :rows_here, :panel_slots] for part in b_parts[1]]
    columns = jnp.stack(tag_parts).reshape(n_row, rows_here, group_count, slot_count)
    group_columns = lax.dynamic_index_in_dim(columns, group, 2, False)
    a_cols = group_columns
    for hop in range(1, n_col):
        pairs = [((r, r // group_count), (r, (r // group_count + hop) % n_col)) for r in range(n_row)]
        a_cols = jnp.where((col - panel) % n_col == hop, send(group_columns, pairs), a_cols)
    a_cols, gathered[1], *arrived = after(a_cols, gathered[1], *own_swapped, *held)
    own_swapped, held = arrived[: group_count - 1], arrived[group_count - 1 :]
    a_cols, b_cols = a_cols.astype(jnp.int32), columns.astype(jnp.int32)
    b_cols = b_cols + width_g * lax.broadcasted_iota(jnp.int32, columns.shape, 2)
    b_cols = b_cols.reshape(n_row, rows_here, panel_slots)
    onehot = a_cols[..., None] == jnp.arange(width_g, dtype=jnp.int32)
    wanted = jnp.sum(jnp.where(onehot[..., None], kept_columns, 0), axis=3)
    match = wanted[..., None] == b_cols[:, :, None, None, :]
    hit = jnp.max(jnp.where(match, jnp.arange(panel_slots, dtype=jnp.int32), -1), axis=-1)
    result = a_cols[..., None] * keep_count + jnp.arange(keep_count, dtype=jnp.int32)
    place = jnp.stack([(panel == col).astype(jnp.int32), group, panel]).astype(jnp.int32)
    codes = []
    for i, j in zip(cuts, cuts[1:]):
        rows_q = jnp.arange(n_row * (j - i), dtype=jnp.int32).reshape(n_row, j - i, 1, 1)
        code = (rows_q * panel_slots + hit[:, i:j]) * (1 << SHIFT) + result[:, i:j]
        codes.append(jnp.where(hit[:, i:j] >= 0, code, -1).reshape(-1))

    out, parts, plans = None, pieces(1), codes[:-1]
    for q in range(len(gathered)):
        a_parts = cores(held, own_swapped)
        if q + 1 < len(gathered):
            arrived = after(*parts, *held[1:])
            held[1:] = arrived[len(chips) :]
            coming = in_plane(q + 1, arrived[: len(chips)])
            own_swapped = own_swaps(q + 1)
        out = add_products(
            cuts[q : q + 2], codes[q].shape[0], plans[q], place, a_parts, [*b_parts[0], *b_parts[1]], out, out_blocks, group_count, slot_count, q + 1 == len(gathered)
        )
        parts = []
        if q + 2 < len(gathered):
            if q == 0:
                out, later = after(out, codes[-1])
                plans += make_plans([later], place, out_blocks, group_count, slot_count, keep_count)
            out, gathered[q + 2], *plans = after(out, gathered[q + 2], *plans)
            parts = pieces(q + 2)
        if q + 1 < len(gathered):
            out, *arrived = after(out, *own_swapped, *parts, *coming[1:])
            own_swapped, arrived = arrived[: group_count - 1], arrived[group_count - 1 :]
            parts, held = arrived[: len(parts)], [coming[0], *arrived[len(parts) :]]
    return out.reshape(width_g, keep_count, block_size, block_size)


def solution(mesh):
    placed = (P("row", "col", None, None, None), P("row", "col", None), P("row", "col"))
    return jax.shard_map(
        on_device,
        mesh=mesh,
        in_specs=placed,
        out_specs=P("row", "col", None, None),
        check_vma=False,
    )
```
